128 devices in a mesh: seq: 32 (over y, z, core), head: 4 (over x).
Axes of the slice: x: 4, y: 4, z: 4, core: 2. Of those that a mesh axis runs over, the one named last changes fastest.
Arguments:
- query_rows: bfloat16 [32768, 5120], P(('seq', 'head')), may hold values from -6 to 6
- key_rows: bfloat16 [32768, 5120], P(('seq', 'head')), may hold values from -6 to 6
- value_rows: bfloat16 [32768, 5120], P(('seq', 'head')), may hold values from -6 to 6
- log_decay: bfloat16 [32768, 40], P(('seq', 'head')), may hold values from -1 to 0
- documents: int32 [32768], replicated, may hold values from 0 to 2, as said below
- norm_gain: float32 [5120], replicated, may hold values from 0.25 to 1.75
Outputs:
- attended: bfloat16 [32768, 5120], P(('seq', 'head'))
The draws below stay inside these ranges and needn't reach their ends.
Inputs may be any that keep to these rules, and one draw needn't show every extreme that they name: `documents`: document numbers never fall along the tokens and each of the 3 numbers occurs.
All inputs are finite; a program needn't handle non-finite values.
Results may differ from the reference program's by a relative error of at most 0.0056.
Values may be sent and summed in bfloat16 or wider, within the bound.
No kernel may reach another device: no remote copies, remote signals or barrier semaphores. Data moves between devices by JAX's collectives and lax.ppermute only.
A program may use at most 640 MiB of HBM per device.

```python
import jax
import jax.numpy as jnp
from jax import lax

HEAD_TOTAL = 40
DH = 128
BLOCK = 256
TOKEN_TOTAL = 32768


def draw_log_decay(key, part):
    key_vectors = jax.random.split(key, 6)
    fast_share = 0.5
    fast_heads = jax.random.uniform(key_vectors[0], (HEAD_TOTAL,)) < fast_share
    fast_rate = jnp.exp(jax.random.uniform(key_vectors[1], (HEAD_TOTAL,), minval=jnp.log(1.0 / 50.0), maxval=jnp.log(1.0 / 30.0)))
    slow_rate = jnp.exp(jax.random.uniform(key_vectors[2], (HEAD_TOTAL,), minval=jnp.log(0.2), maxval=jnp.log(0.6))) / TOKEN_TOTAL
    baseline_decay_rate = jnp.where(fast_heads, fast_rate, slow_rate)
    decay_spread = jnp.exp(jax.random.uniform(key_vectors[3], (TOKEN_TOTAL // 64, HEAD_TOTAL), minval=jnp.log(0.5), maxval=jnp.log(2.0)))
    decay_spread = jnp.repeat(decay_spread, 64, axis=0)
    reset_positions = jax.random.uniform(key_vectors[4], (TOKEN_TOTAL, HEAD_TOTAL)) < 3.0 / TOKEN_TOTAL
    decay_strength = jnp.log(jax.random.uniform(key_vectors[5], (TOKEN_TOTAL, HEAD_TOTAL), minval=0.5, maxval=0.8))
    value_vectors = -baseline_decay_rate[None, :] * decay_spread + jnp.where(reset_positions, decay_strength, 0.0)
    return value_vectors.astype(jnp.float32).astype(jnp.bfloat16)


def draw_documents(key, part):
    first_key = jax.random.fold_in(key, 11)
    second_key = jax.random.fold_in(key, 12)
    first_bound = jax.random.randint(first_key, (), TOKEN_TOTAL // 8, TOKEN_TOTAL // 4)
    second_bound = jax.random.randint(second_key, (), 3 * TOKEN_TOTAL // 4, 7 * TOKEN_TOTAL // 8)
    positions = jnp.arange(TOKEN_TOTAL, dtype=jnp.int32)
    return (positions >= first_bound).astype(jnp.int32) + (positions >= second_bound).astype(jnp.int32)


def shard_levels(key, dims, cuts, low, top_value):
    factor_of, own = 1.0, jax.random.fold_in(key, 6)
    for axis_at, parts in cuts:
        steps = jnp.exp(jax.random.uniform(jax.random.fold_in(own, axis_at), (parts,), jnp.float32, low / len(cuts), top_value / len(cuts)))
        factor_of = factor_of * jnp.repeat(steps, dims[axis_at] // parts).reshape([-1 if axis == axis_at else 1 for axis in range(len(dims))])
    return factor_of


def normal_values(rng, shape, scale, reach, pieces=(), held_as=jnp.bfloat16):
    result = jax.random.normal(rng, shape, jnp.float32) * scale
    if len(pieces) > 0:
        result = shard_levels(rng, shape, pieces, -0.22, 0.18) * result
    return jnp.clip(result, min=-reach, max=reach).astype(held_as)


def setup_inputs(seed: int = 0) -> dict:
    seeds = jax.random.split(jax.random.key(seed), 7)
    return {
        "query_rows": normal_values(seeds[0], (TOKEN_TOTAL, HEAD_TOTAL * DH), 1.0, 6.0, ((0, 128),)),
        "key_rows": normal_values(seeds[1], (TOKEN_TOTAL, HEAD_TOTAL * DH), 1.0, 6.0, ((0, 128),)),
        "value_rows": normal_values(seeds[2], (TOKEN_TOTAL, HEAD_TOTAL * DH), 1.0, 6.0, ((0, 128),)),
        "log_decay": draw_log_decay(jax.random.fold_in(seeds[6], 71), 0),
        "documents": draw_documents(jax.random.fold_in(seeds[6], 71), 0),
        "norm_gain": jnp.clip(1.0 + 0.15 * jax.random.normal(seeds[5], (HEAD_TOTAL * DH,), jnp.float32), 0.25, 1.75),
    }


def to_bfloat(value_vectors):
    return lax.optimization_barrier(value_vectors.astype(jnp.bfloat16)).astype(jnp.float32)

def reference(query_rows, key_rows, value_rows, log_decay, documents, norm_gain):
    block_count = TOKEN_TOTAL // BLOCK
    query_blocks = query_rows.reshape(block_count, BLOCK, HEAD_TOTAL, DH)
    key_blocks = key_rows.reshape(block_count, BLOCK, HEAD_TOTAL, DH)
    value_blocks = value_rows.reshape(block_count, BLOCK, HEAD_TOTAL, DH)
    cumulative = jnp.cumsum(log_decay.astype(jnp.float32).reshape(block_count, BLOCK, HEAD_TOTAL), axis=1)
    doc_blocks = documents.reshape(block_count, BLOCK)
    previous = jnp.concatenate([documents[:1], doc_blocks[:-1, -1]])
    causal = jnp.arange(BLOCK)[:, None] >= jnp.arange(BLOCK)[None, :]

    def advance(carried_state, item):
        query_one, key_one, value_one, cum_one, doc_one, prev_one = item
        query_f = query_one.astype(jnp.float32)
        key_f = key_one.astype(jnp.float32)
        value_f = value_one.astype(jnp.float32)
        scores = jnp.einsum('chd,shd->hcs', query_f, key_f)
        cum_heads = cum_one.T
        exponent = cum_heads[:, :, None] - cum_heads[:, None, :]
        allowed = (causal & (doc_one[:, None] == doc_one[None, :]))[None]
        decay_mask = jnp.where(allowed, jnp.exp(jnp.where(allowed, exponent, 0.0)), 0.0)
        weights = to_bfloat(scores * decay_mask)
        within = jnp.einsum('hcs,shd->chd', weights, value_f)
        usable = (doc_one == prev_one).astype(jnp.float32)
        query_decayed = to_bfloat(query_f * (jnp.exp(cum_one) * usable[:, None])[:, :, None])
        carried = jnp.einsum('chd,hde->che', query_decayed, to_bfloat(carried_state))
        final_cum = cum_one[-1]
        same_last = (doc_one == doc_one[-1]).astype(jnp.float32)
        key_decayed = to_bfloat(key_f * (jnp.exp(final_cum[None, :] - cum_one) * same_last[:, None])[:, :, None])
        update = jnp.einsum('chd,che->hde', key_decayed, value_f)
        factor = jnp.exp(final_cum) * (doc_one[-1] == prev_one).astype(jnp.float32)
        return (factor[:, None, None] * carried_state + update, within + carried)
    start_state = jnp.zeros((HEAD_TOTAL, DH, DH), jnp.float32)
    _, outputs = lax.scan(advance, start_state, (query_blocks, key_blocks, value_blocks, cumulative, doc_blocks, previous))
    mean_square = lax.optimization_barrier(jnp.mean(outputs * outputs, axis=-1, keepdims=True))
    normed = outputs * lax.rsqrt(mean_square + 1e-05) * norm_gain.reshape(HEAD_TOTAL, DH)
    return normed.astype(jnp.bfloat16).reshape(TOKEN_TOTAL, HEAD_TOTAL * DH)
```

```python
import functools

import jax
import jax.numpy as jnp
from jax import lax
from jax.experimental import pallas as pl
from jax.experimental.pallas import tpu as pltpu
from jax.sharding import PartitionSpec as P

BLOCK = 256
DH = 128
HEADS = 40
GROUPS = 8
PER = HEADS // GROUPS
SLABS = 16
DEVICES = GROUPS * SLABS
F32 = jnp.float32
BF16 = jnp.bfloat16
VMEM = 58 << 20


def doc_row(docs_ref, block):
    rows = docs_ref[pl.ds(2 * block, 2), :]
    row = jnp.concatenate([rows[0:1], rows[1:2]], axis=1)
    before = docs_ref[pl.ds(jnp.maximum(2 * block - 1, 0), 1), :]
    prev = jnp.where(block == 0, row[:, 0:1], before[:, DH - 1 : DH])
    return row, prev


def lower_ones():
    t = lax.broadcasted_iota(jnp.int32, (BLOCK, BLOCK), 0)
    s = lax.broadcasted_iota(jnp.int32, (BLOCK, BLOCK), 1)
    return t >= s


def cum_rows(decay):
    tri = lower_ones().astype(F32).astype(BF16)
    return lax.dot_general(decay, tri, (((1,), (1,)), ((), ())), preferred_element_type=F32)


def state_kernel(block_ref, key_ref, value_ref, decay_ref, docs_ref, out_ref, scale_ref, factor_ref):
    group = pl.program_id(0)

    @pl.when(group == 0)
    def _():
        row, prev = doc_row(docs_ref, block_ref[0])
        last = row[:, BLOCK - 1 : BLOCK]
        cum = cum_rows(decay_ref[...])
        final = cum[:, BLOCK - 1 : BLOCK]
        same = (row == last).astype(F32)
        scale_ref[...] = jnp.exp(final - cum) * same
        factor = jnp.exp(final) * (last == prev).astype(F32)
        factor = jnp.broadcast_to(factor, (HEADS, DH))
        high = factor.astype(BF16).astype(F32)
        middle = (factor - high).astype(BF16).astype(F32)
        low = factor - high - middle
        lane = lax.broadcasted_iota(jnp.int32, (HEADS, DH), 1)
        parts = jnp.where(lane == 0, high, jnp.where(lane == 1, middle, jnp.where(lane == 2, low, 0.0)))
        factor_ref[0:HEADS, :] = parts
        factor_ref[HEADS:, :] = jnp.zeros((8, DH), F32)

    for one in range(PER):
        cols = slice(one * DH, (one + 1) * DH)
        keys = key_ref[:, cols].T.astype(F32)
        decayed = (keys * scale_ref[pl.ds(group * PER + one, 1), :]).astype(BF16)
        update = jnp.dot(decayed, value_ref[:, cols], preferred_element_type=F32)
        out_ref[:, one] = update.reshape(SLABS, 8, DH).astype(BF16)
    parts = factor_ref[pl.ds(group * PER, 8), :].astype(BF16)
    out_ref[:, PER] = jnp.broadcast_to(parts[None], (SLABS, 8, DH))


def scan_kernel(update_ref, out_ref, carry_ref):
    step = pl.program_id(0)

    @pl.when(step == 0)
    def _():
        carry_ref[...] = jnp.zeros_like(carry_ref)

    state = [carry_ref[one] for one in range(PER)]
    for b in range(update_ref.shape[0]):
        factors = jnp.sum(update_ref[b, PER].astype(F32), axis=1, keepdims=True)
        for one in range(PER):
            out_ref[b, one] = state[one].astype(BF16)
            state[one] = factors[one : one + 1] * state[one] + update_ref[b, one].astype(F32)
    for one in range(PER):
        carry_ref[one] = state[one]


def local_kernel(
    block_ref, query_ref, key_ref, value_ref, decay_ref, docs_ref, within_ref, decayed_ref, row_ref, col_ref, use_ref, mask_ref
):
    group = pl.program_id(0)

    @pl.when(group == 0)
    def _():
        row, prev = doc_row(docs_ref, block_ref[0])
        decay = decay_ref[...]
        row_ref[...] = cum_rows(decay)
        lower = lower_ones()
        ones = lower.astype(F32).astype(BF16)
        cum = lax.dot_general(ones, decay, (((1,), (1,)), ((), ())), preferred_element_type=F32)
        rows = jnp.broadcast_to(row.astype(F32), (BLOCK, BLOCK))
        cols = rows.T
        mask_ref[...] = (lower & (rows == cols)).astype(F32)
        usable = (cols[:, 0:1] == prev.astype(F32)).astype(F32)
        use = jnp.exp(cum) * usable
        for g in range(GROUPS):
            col_ref[g] = cum[:, g * PER : (g + 1) * PER]
            use_ref[g] = use[:, g * PER : (g + 1) * PER]

    allowed = mask_ref[...] > 0.5
    for one in range(PER):
        cols = slice(one * DH, (one + 1) * DH)
        query = query_ref[:, cols]
        scores = lax.dot_general(query, key_ref[:, cols], (((1,), (1,)), ((), ())), preferred_element_type=F32)
        exponent = col_ref[group, :, one : one + 1] - row_ref[pl.ds(group * PER + one, 1), :]
        mask = jnp.exp(jnp.where(allowed, exponent, -jnp.inf))
        weights = (scores * mask).astype(BF16)
        within_ref[:, cols] = jnp.dot(weights, value_ref[:, cols], preferred_element_type=F32)
        decayed_ref[:, cols] = (query.astype(F32) * use_ref[group, :, one : one + 1]).astype(BF16)


def finish_kernel(decayed_ref, state_ref, within_ref, gain_ref, out_ref):
    for one in range(PER):
        cols = slice(one * DH, (one + 1) * DH)
        state = state_ref[:, one].reshape(DH, DH)
        total = within_ref[:, cols] + jnp.dot(decayed_ref[:, cols], state, preferred_element_type=F32)
        square = jnp.mean(total * total, axis=1, keepdims=True)
        out_ref[:, cols] = (total * lax.rsqrt(square + 1e-05) * gain_ref[:, cols]).astype(BF16)


def body(query, keyed, valued, decay, documents, gain):
    axes = ("seq", "head")
    block = lax.axis_index(axes).astype(jnp.int32).reshape(1)
    docs = documents.reshape(-1, DH)
    gain = gain.reshape(1, -1)
    decay = decay.T
    wide = PER * DH
    rows = pl.BlockSpec((BLOCK, wide), lambda g, *_: (0, g))
    whole = lambda a: pl.BlockSpec(a.shape, lambda g, *_: (0,) * a.ndim)

    update = pl.pallas_call(
        state_kernel,
        grid_spec=pltpu.PrefetchScalarGridSpec(
            num_scalar_prefetch=1,
            grid=(GROUPS,),
            in_specs=[rows, rows, whole(decay), whole(docs)],
            out_specs=pl.BlockSpec((SLABS, PER + 1, 8, DH), lambda g, *_: (g, 0, 0, 0)),
            scratch_shapes=[pltpu.VMEM((HEADS, BLOCK), F32), pltpu.VMEM((HEADS + 8, DH), F32)],
        ),
        out_shape=jax.ShapeDtypeStruct((DEVICES, PER + 1, 8, DH), BF16),
        compiler_params=pltpu.CompilerParams(vmem_limit_bytes=VMEM),
        cost_estimate=pl.CostEstimate(flops=340_000_000, bytes_accessed=7_000_000, transcendentals=10_000),
        name="state_update",
    )(block, keyed, valued, decay, docs)

    moved = lax.all_to_all(update, axes, split_axis=0, concat_axis=0, tiled=True)

    within, decayed = pl.pallas_call(
        local_kernel,
        grid_spec=pltpu.PrefetchScalarGridSpec(
            num_scalar_prefetch=1,
            grid=(GROUPS,),
            in_specs=[rows, rows, rows, whole(decay), whole(docs)],
            out_specs=[rows, rows],
            scratch_shapes=[
                pltpu.VMEM((HEADS, BLOCK), F32),
                pltpu.VMEM((GROUPS, BLOCK, PER), F32),
                pltpu.VMEM((GROUPS, BLOCK, PER), F32),
                pltpu.VMEM((BLOCK, BLOCK), F32),
            ],
        ),
        out_shape=[jax.ShapeDtypeStruct(query.shape, F32), jax.ShapeDtypeStruct(query.shape, BF16)],
        compiler_params=pltpu.CompilerParams(vmem_limit_bytes=VMEM),
        cost_estimate=pl.CostEstimate(flops=1_400_000_000, bytes_accessed=16_000_000, transcendentals=2_700_000),
        name="local_attention",
    )(block, query, keyed, valued, decay, docs)

    chunk = 16
    states = pl.pallas_call(
        scan_kernel,
        grid=(DEVICES // chunk,),
        in_specs=[pl.BlockSpec((chunk, PER + 1, 8, DH), lambda b: (b, 0, 0, 0))],
        out_specs=pl.BlockSpec((chunk, PER, 8, DH), lambda b: (b, 0, 0, 0)),
        out_shape=jax.ShapeDtypeStruct((DEVICES, PER, 8, DH), BF16),
        scratch_shapes=[pltpu.VMEM((PER, 8, DH), F32)],
        compiler_params=pltpu.CompilerParams(vmem_limit_bytes=VMEM),
        name="block_scan",
    )(moved)

    entering = lax.all_to_all(states, axes, split_axis=0, concat_axis=0, tiled=True)

    return pl.pallas_call(
        finish_kernel,
        grid=(GROUPS,),
        in_specs=[
            rows,
            pl.BlockSpec((SLABS, PER, 8, DH), lambda g: (g, 0, 0, 0)),
            rows,
            pl.BlockSpec((1, wide), lambda g: (0, g)),
        ],
        out_specs=rows,
        out_shape=jax.ShapeDtypeStruct(query.shape, BF16),
        compiler_params=pltpu.CompilerParams(vmem_limit_bytes=VMEM),
        name="finish",
    )(decayed, entering, within, gain)


def solution(mesh):
    placed = P(("seq", "head"), None)
    return jax.shard_map(
        body, mesh=mesh, in_specs=(placed, placed, placed, placed, P(), P()), out_specs=placed, check_vma=False
    )
```

```python
import functools

import jax
import jax.numpy as jnp
from jax import lax
from jax.experimental import pallas as pl
from jax.experimental.pallas import tpu as pltpu
from jax.sharding import PartitionSpec as P

BLOCK = 256
DH = 128
HEADS = 40
GROUPS = 8
PER = HEADS // GROUPS
SLABS = 16
DEVICES = GROUPS * SLABS
STEP_GROUPS = 4
F32 = jnp.float32
BF16 = jnp.bfloat16
VMEM = 58 << 20


def doc_row(docs_ref, block):
    rows = docs_ref[pl.ds(2 * block, 2), :]
    row = jnp.concatenate([rows[0:1], rows[1:2]], axis=1)
    before = docs_ref[pl.ds(jnp.maximum(2 * block - 1, 0), 1), :]
    prev = jnp.where(block == 0, row[:, 0:1], before[:, DH - 1 : DH])
    return row, prev


def lower_ones():
    t = lax.broadcasted_iota(jnp.int32, (BLOCK, BLOCK), 0)
    s = lax.broadcasted_iota(jnp.int32, (BLOCK, BLOCK), 1)
    return t >= s


def cum_rows(decay):
    tri = lower_ones().astype(F32).astype(BF16)
    return lax.dot_general(decay, tri, (((1,), (1,)), ((), ())), preferred_element_type=F32)


def state_kernel(block_ref, key_ref, value_ref, decay_ref, docs_ref, out_ref, scale_ref, factor_ref):
    step = pl.program_id(0)

    @pl.when(step == 0)
    def _():
        row, prev = doc_row(docs_ref, block_ref[0])
        last = row[:, BLOCK - 1 : BLOCK]
        cum = cum_rows(decay_ref[...])
        final = cum[:, BLOCK - 1 : BLOCK]
        same = (row == last).astype(F32)
        scale_ref[...] = jnp.exp(final - cum) * same
        factor = jnp.exp(final) * (last == prev).astype(F32)
        factor = jnp.broadcast_to(factor, (HEADS, DH))
        high = factor.astype(BF16).astype(F32)
        middle = (factor - high).astype(BF16).astype(F32)
        low = factor - high - middle
        lane = lax.broadcasted_iota(jnp.int32, (HEADS, DH), 1)
        parts = jnp.where(lane == 0, high, jnp.where(lane == 1, middle, jnp.where(lane == 2, low, 0.0)))
        factor_ref[0:HEADS, :] = parts
        factor_ref[HEADS:, :] = jnp.zeros((8, DH), F32)

    for sub in range(STEP_GROUPS):
        first = (step * STEP_GROUPS + sub) * PER
        slabs = slice(sub * SLABS, (sub + 1) * SLABS)
        for one in range(PER):
            cols = slice((sub * PER + one) * DH, (sub * PER + one + 1) * DH)
            keys = key_ref[:, cols].T.astype(F32)
            decayed = (keys * scale_ref[pl.ds(first + one, 1), :]).astype(BF16)
            update = jnp.dot(decayed, value_ref[:, cols], preferred_element_type=F32)
            out_ref[slabs, one] = update.reshape(SLABS, 8, DH).astype(BF16)
        parts = factor_ref[pl.ds(first, 8), :].astype(BF16)
        out_ref[slabs, PER] = jnp.broadcast_to(parts[None], (SLABS, 8, DH))


def scan_kernel(update_ref, decayed_hbm, out_ref, decayed_ref, sem):
    fetch = pltpu.make_async_copy(decayed_hbm, decayed_ref, sem)
    fetch.start()
    state = [jnp.zeros((8, DH), F32) for _ in range(PER)]
    for b in range(DEVICES):
        factors = jnp.sum(update_ref[b, PER].astype(F32), axis=1, keepdims=True)
        for one in range(PER):
            out_ref[b, one] = state[one].astype(BF16)
            state[one] = factors[one : one + 1] * state[one] + update_ref[b, one].astype(F32)
    fetch.wait()


def local_kernel(
    block_ref, query_ref, key_ref, value_ref, decay_ref, docs_ref, within_ref, decayed_ref, row_ref, col_ref, use_ref, mask_ref
):
    group = pl.program_id(0)

    @pl.when(group == 0)
    def _():
        row, prev = doc_row(docs_ref, block_ref[0])
        decay = decay_ref[...]
        row_ref[...] = cum_rows(decay)
        lower = lower_ones()
        ones = lower.astype(F32).astype(BF16)
        cum = lax.dot_general(ones, decay, (((1,), (1,)), ((), ())), preferred_element_type=F32)
        rows = jnp.broadcast_to(row.astype(F32), (BLOCK, BLOCK))
        cols = rows.T
        mask_ref[...] = (lower & (rows == cols)).astype(F32)
        usable = (cols[:, 0:1] == prev.astype(F32)).astype(F32)
        use = jnp.exp(cum) * usable
        for g in range(GROUPS):
            col_ref[g] = cum[:, g * PER : (g + 1) * PER]
            use_ref[g] = use[:, g * PER : (g + 1) * PER]

    allowed = mask_ref[...] > 0.5
    for one in range(PER):
        cols = slice(one * DH, (one + 1) * DH)
        query = query_ref[:, cols]
        scores = lax.dot_general(query, key_ref[:, cols], (((1,), (1,)), ((), ())), preferred_element_type=F32)
        exponent = col_ref[group, :, one : one + 1] - row_ref[pl.ds(group * PER + one, 1), :]
        mask = jnp.exp(jnp.where(allowed, exponent, -jnp.inf))
        weights = (scores * mask).astype(BF16)
        within_ref[:, cols] = jnp.dot(weights, value_ref[:, cols], preferred_element_type=F32)
        decayed_ref[:, cols] = (query.astype(F32) * use_ref[group, :, one : one + 1]).astype(BF16)


def finish_kernel(decayed_ref, state_ref, within_ref, gain_ref, out_hbm, out_ref, sems):
    copies = []
    for g in range(GROUPS):
        for one in range(g * PER, (g + 1) * PER):
            cols = slice(one * DH, (one + 1) * DH)
            state = state_ref[g * SLABS : (g + 1) * SLABS, one - g * PER].reshape(DH, DH)
            carried = jnp.dot(decayed_ref[:, cols], state, preferred_element_type=F32)
            total = within_ref[:, cols] + carried
            square = jnp.mean(total * total, axis=1, keepdims=True)
            out_ref[:, cols] = (total * lax.rsqrt(square + 1e-05) * gain_ref[:, cols]).astype(BF16)
        cols = slice(g * PER * DH, (g + 1) * PER * DH)
        copies.append(pltpu.make_async_copy(out_ref.at[:, cols], out_hbm.at[:, cols], sems.at[g]))
        copies[-1].start()
    for copy in copies:
        copy.wait()


def body(query, keyed, valued, decay, documents, gain):
    axes = ("seq", "head")
    block = lax.axis_index(axes).astype(jnp.int32).reshape(1)
    docs = documents.reshape(-1, DH)
    gain = gain.reshape(1, -1)
    decay = decay.T
    wide = PER * DH
    rows = pl.BlockSpec((BLOCK, wide), lambda g, *_: (0, g))
    whole = lambda a: pl.BlockSpec(a.shape, lambda g, *_: (0,) * a.ndim)

    wider = pl.BlockSpec((BLOCK, STEP_GROUPS * wide), lambda g, *_: (0, g))
    update = pl.pallas_call(
        state_kernel,
        grid_spec=pltpu.PrefetchScalarGridSpec(
            num_scalar_prefetch=1,
            grid=(GROUPS // STEP_GROUPS,),
            in_specs=[wider, wider, whole(decay), whole(docs)],
            out_specs=pl.BlockSpec((STEP_GROUPS * SLABS, PER + 1, 8, DH), lambda g, *_: (g, 0, 0, 0)),
            scratch_shapes=[pltpu.VMEM((HEADS, BLOCK), F32), pltpu.VMEM((HEADS + 8, DH), F32)],
        ),
        out_shape=jax.ShapeDtypeStruct((DEVICES, PER + 1, 8, DH), BF16),
        compiler_params=pltpu.CompilerParams(vmem_limit_bytes=VMEM),
        cost_estimate=pl.CostEstimate(flops=340_000_000, bytes_accessed=7_000_000, transcendentals=10_000),
        name="state_update",
    )(block, keyed, valued, decay, docs)

    moved = lax.all_to_all(update, axes, split_axis=0, concat_axis=0, tiled=True)

    within, decayed = pl.pallas_call(
        local_kernel,
        grid_spec=pltpu.PrefetchScalarGridSpec(
            num_scalar_prefetch=1,
            grid=(GROUPS,),
            in_specs=[rows, rows, rows, whole(decay), whole(docs)],
            out_specs=[rows, rows],
            scratch_shapes=[
                pltpu.VMEM((HEADS, BLOCK), F32),
                pltpu.VMEM((GROUPS, BLOCK, PER), F32),
                pltpu.VMEM((GROUPS, BLOCK, PER), F32),
                pltpu.VMEM((BLOCK, BLOCK), F32),
            ],
        ),
        out_shape=[jax.ShapeDtypeStruct(query.shape, F32), jax.ShapeDtypeStruct(query.shape, BF16)],
        compiler_params=pltpu.CompilerParams(vmem_limit_bytes=VMEM),
        cost_estimate=pl.CostEstimate(flops=1_400_000_000, bytes_accessed=16_000_000, transcendentals=2_700_000),
        name="local_attention",
    )(block, query, keyed, valued, decay, docs)

    moved, within, decayed = lax.optimization_barrier((moved, within, decayed))
    vmem = pl.BlockSpec(memory_space=pltpu.VMEM)
    states, decayed = pl.pallas_call(
        scan_kernel,
        in_specs=[vmem, pl.BlockSpec(memory_space=pltpu.HBM)],
        out_specs=[vmem, vmem],
        out_shape=[jax.ShapeDtypeStruct((DEVICES, PER, 8, DH), BF16), jax.ShapeDtypeStruct(query.shape, BF16)],
        scratch_shapes=[pltpu.SemaphoreType.DMA],
        compiler_params=pltpu.CompilerParams(vmem_limit_bytes=8 << 20),
        name="block_scan",
    )(moved, pltpu.with_memory_space_constraint(decayed, pltpu.HBM))

    entering = lax.all_to_all(states, axes, split_axis=0, concat_axis=0, tiled=True)

    return pl.pallas_call(
        finish_kernel,
        in_specs=[vmem] * 4,
        out_specs=pl.BlockSpec(memory_space=pl.ANY),
        out_shape=jax.ShapeDtypeStruct(query.shape, BF16),
        scratch_shapes=[pltpu.VMEM(query.shape, BF16), pltpu.SemaphoreType.DMA((GROUPS,))],
        compiler_params=pltpu.CompilerParams(vmem_limit_bytes=16 << 20),
        name="finish",
    )(decayed, entering, within, gain)


def solution(mesh):
    placed = P(("seq", "head"), None)
    return jax.shard_map(
        body, mesh=mesh, in_specs=(placed, placed, placed, placed, P(), P()), out_specs=placed, check_vma=False
    )
```

```python
import functools

import jax
import jax.numpy as jnp
from jax import lax
from jax.experimental import pallas as pl
from jax.experimental.pallas import tpu as pltpu
from jax.sharding import PartitionSpec as P

BLOCK = 256
DH = 128
HEADS = 40
GROUPS = 8
PER = HEADS // GROUPS
SLABS = 16
DEVICES = GROUPS * SLABS
STEP_GROUPS = 4
ROWS = PER * 8 + 2


def member_order():
    order = []
    for i in range(DEVICES):
        bit = [(i >> k) & 1 for k in range(7)]
        x, y, z = (bit[k] + 2 * bit[k + 4] for k in range(3))
        order.append(((y * 4 + z) * 2 + bit[3]) * 4 + x)
    return order


ORDER = member_order()
F32 = jnp.float32
BF16 = jnp.bfloat16
VMEM = 58 << 20


def doc_row(docs_ref, block):
    rows = docs_ref[pl.ds(2 * block, 2), :]
    row = jnp.concatenate([rows[0:1], rows[1:2]], axis=1)
    before = docs_ref[pl.ds(jnp.maximum(2 * block - 1, 0), 1), :]
    prev = jnp.where(block == 0, row[:, 0:1], before[:, DH - 1 : DH])
    return row, prev


def lower_ones():
    t = lax.broadcasted_iota(jnp.int32, (BLOCK, BLOCK), 0)
    s = lax.broadcasted_iota(jnp.int32, (BLOCK, BLOCK), 1)
    return t >= s


def cum_rows(decay):
    tri = lower_ones().astype(F32).astype(BF16)
    return lax.dot_general(decay, tri, (((1,), (1,)), ((), ())), preferred_element_type=F32)


def state_kernel(block_ref, key_ref, value_ref, decay_ref, docs_ref, out_ref, scale_ref, wide_ref):
    step = pl.program_id(0)

    @pl.when(step == 0)
    def _():
        row, prev = doc_row(docs_ref, block_ref[0])
        last = row[:, BLOCK - 1 : BLOCK]
        decay = decay_ref[...]
        cum = cum_rows(decay)
        final = cum[:, BLOCK - 1 : BLOCK]
        same = (row == last).astype(F32)
        scale_ref[...] = jnp.exp(final - cum) * same
        ones = jnp.ones((8, BLOCK), BF16)
        final = lax.dot_general(ones, decay, (((1,), (1,)), ((), ())), preferred_element_type=F32)
        factor = jnp.exp(final) * (last == prev).astype(F32)
        high = factor.astype(BF16).astype(F32)
        middle = (factor - high).astype(BF16).astype(F32)
        low = factor - high - middle
        parts = jnp.concatenate([high, middle, low, jnp.zeros((8, DH - 3 * HEADS), F32)], axis=1)
        for piece in range(STEP_GROUPS * SLABS):
            wide_ref[(piece + 1) * ROWS - 2 : (piece + 1) * ROWS, :] = parts[0:2]

    for sub in range(STEP_GROUPS):
        first = (step * STEP_GROUPS + sub) * PER
        start = sub * SLABS * ROWS
        for one in range(PER):
            cols = slice((sub * PER + one) * DH, (sub * PER + one + 1) * DH)
            keys = key_ref[:, cols].T.astype(F32)
            decayed = (keys * scale_ref[pl.ds(first + one, 1), :]).astype(BF16)
            update = jnp.dot(decayed, value_ref[:, cols], preferred_element_type=F32)
            for slab in range(SLABS):
                at = start + slab * ROWS + one * 8
                wide_ref[at : at + 8, :] = update[slab * 8 : (slab + 1) * 8]
        rows = slice(start, start + SLABS * ROWS)
        out_ref[rows, :] = wide_ref[rows, :].astype(BF16)


def scan_kernel(block_ref, update_ref, decayed_hbm, out_ref, decayed_ref, wide_ref, factor_ref, sem):
    fetch = pltpu.make_async_copy(decayed_hbm, decayed_ref, sem)
    fetch.start()
    for g in range(GROUPS):
        rows = slice(g * SLABS * ROWS, (g + 1) * SLABS * ROWS)
        wide_ref[rows, :] = update_ref[rows, :].astype(F32)
    block = block_ref[0]
    group = ((block >> 1) & 1) + 2 * ((block >> 6) & 1) + 4 * ((block >> 4) & 1)
    parts = wide_ref[pl.ds(ROWS - 2, DEVICES, stride=ROWS), :].astype(BF16)
    lane = lax.broadcasted_iota(jnp.int32, (DH, DH), 0)
    for one in range(PER):
        head = group * PER + one
        pick = (lane == head) | (lane == head + HEADS) | (lane == head + 2 * HEADS)
        factor_ref[one] = jnp.dot(parts, pick.astype(F32).astype(BF16), preferred_element_type=F32)
    state = [jnp.zeros((8, DH), F32) for _ in range(PER)]
    for b in range(DEVICES):
        place = ORDER.index(b)
        for one in range(PER):
            at = place * ROWS + one * 8
            out_ref[place, one] = state[one].astype(BF16)
            state[one] = factor_ref[one, place : place + 1, :] * state[one] + wide_ref[at : at + 8, :]
    fetch.wait()


def local_kernel(
    block_ref, query_ref, key_ref, value_ref, decay_ref, docs_ref, within_ref, decayed_ref, row_ref, col_ref, use_ref, mask_ref
):
    group = pl.program_id(0)

    @pl.when(group == 0)
    def _():
        row, prev = doc_row(docs_ref, block_ref[0])
        decay = decay_ref[...]
        row_ref[...] = cum_rows(decay)
        lower = lower_ones()
        ones = lower.astype(F32).astype(BF16)
        cum = lax.dot_general(ones, decay, (((1,), (1,)), ((), ())), preferred_element_type=F32)
        rows = jnp.broadcast_to(row.astype(F32), (BLOCK, BLOCK))
        cols = rows.T
        mask_ref[...] = (lower & (rows == cols)).astype(F32)
        usable = (cols[:, 0:1] == prev.astype(F32)).astype(F32)
        use = jnp.exp(cum) * usable
        for g in range(GROUPS):
            col_ref[g] = cum[:, g * PER : (g + 1) * PER]
            use_ref[g] = use[:, g * PER : (g + 1) * PER]

    allowed = mask_ref[...] > 0.5
    for one in range(PER):
        cols = slice(one * DH, (one + 1) * DH)
        query = query_ref[:, cols]
        scores = lax.dot_general(query, key_ref[:, cols], (((1,), (1,)), ((), ())), preferred_element_type=F32)
        exponent = col_ref[group, :, one : one + 1] - row_ref[pl.ds(group * PER + one, 1), :]
        mask = jnp.exp(jnp.where(allowed, exponent, -jnp.inf))
        weights = (scores * mask).astype(BF16)
        within_ref[:, cols] = jnp.dot(weights, value_ref[:, cols], preferred_element_type=F32)
        decayed_ref[:, cols] = (query.astype(F32) * use_ref[group, :, one : one + 1]).astype(BF16)


def finish_kernel(decayed_ref, state_ref, within_ref, gain_ref, out_hbm, out_ref, sems):
    copies = []
    for g in range(GROUPS):
        for one in range(g * PER, (g + 1) * PER):
            cols = slice(one * DH, (one + 1) * DH)
            state = state_ref[g * SLABS : (g + 1) * SLABS, one - g * PER].reshape(DH, DH)
            carried = jnp.dot(decayed_ref[:, cols], state, preferred_element_type=F32)
            total = within_ref[:, cols] + carried
            square = jnp.mean(total * total, axis=1, keepdims=True)
            out_ref[:, cols] = (total * lax.rsqrt(square + 1e-05) * gain_ref[:, cols]).astype(BF16)
        cols = slice(g * PER * DH, (g + 1) * PER * DH)
        copies.append(pltpu.make_async_copy(out_ref.at[:, cols], out_hbm.at[:, cols], sems.at[g]))
        copies[-1].start()
    for copy in copies:
        copy.wait()


def body(query, keyed, valued, decay, documents, gain):
    axes = ("seq", "head")
    block = lax.axis_index(axes).astype(jnp.int32).reshape(1)
    docs = documents.reshape(-1, DH)
    gain = gain.reshape(1, -1)
    decay = decay.T
    wide = PER * DH
    rows = pl.BlockSpec((BLOCK, wide), lambda g, *_: (0, g))
    whole = lambda a: pl.BlockSpec(a.shape, lambda g, *_: (0,) * a.ndim)

    wider = pl.BlockSpec((BLOCK, STEP_GROUPS * wide), lambda g, *_: (0, g))
    step_rows = STEP_GROUPS * SLABS * ROWS
    update = pl.pallas_call(
        state_kernel,
        grid_spec=pltpu.PrefetchScalarGridSpec(
            num_scalar_prefetch=1,
            grid=(GROUPS // STEP_GROUPS,),
            in_specs=[wider, wider, whole(decay), whole(docs)],
            out_specs=pl.BlockSpec((step_rows, DH), lambda g, *_: (g, 0)),
            scratch_shapes=[pltpu.VMEM((HEADS, BLOCK), F32), pltpu.VMEM((step_rows, DH), F32)],
        ),
        out_shape=jax.ShapeDtypeStruct((DEVICES * ROWS, DH), BF16),
        compiler_params=pltpu.CompilerParams(vmem_limit_bytes=VMEM),
        cost_estimate=pl.CostEstimate(flops=340_000_000, bytes_accessed=7_000_000, transcendentals=10_000),
        name="state_update",
    )(block, keyed, valued, decay, docs)

    def exchange(pieces):
        return lax.all_to_all(
            pieces, axes, split_axis=0, concat_axis=0, axis_index_groups=[ORDER], tiled=True
        )

    moved = exchange(update.reshape(DEVICES, ROWS // 2, 2, DH)).reshape(DEVICES * ROWS, DH)

    within, decayed = pl.pallas_call(
        local_kernel,
        grid_spec=pltpu.PrefetchScalarGridSpec(
            num_scalar_prefetch=1,
            grid=(GROUPS,),
            in_specs=[rows, rows, rows, whole(decay), whole(docs)],
            out_specs=[rows, rows],
            scratch_shapes=[
                pltpu.VMEM((HEADS, BLOCK), F32),
                pltpu.VMEM((GROUPS, BLOCK, PER), F32),
                pltpu.VMEM((GROUPS, BLOCK, PER), F32),
                pltpu.VMEM((BLOCK, BLOCK), F32),
            ],
        ),
        out_shape=[jax.ShapeDtypeStruct(query.shape, F32), jax.ShapeDtypeStruct(query.shape, BF16)],
        compiler_params=pltpu.CompilerParams(vmem_limit_bytes=VMEM),
        cost_estimate=pl.CostEstimate(flops=1_400_000_000, bytes_accessed=16_000_000, transcendentals=2_700_000),
        name="local_attention",
    )(block, query, keyed, valued, decay, docs)

    moved, within, decayed = lax.optimization_barrier((moved, within, decayed))
    vmem = pl.BlockSpec(memory_space=pltpu.VMEM)
    states, decayed = pl.pallas_call(
        scan_kernel,
        in_specs=[pl.BlockSpec(memory_space=pltpu.SMEM), vmem, pl.BlockSpec(memory_space=pltpu.HBM)],
        out_specs=[vmem, vmem],
        out_shape=[jax.ShapeDtypeStruct((DEVICES, PER, 8, DH), BF16), jax.ShapeDtypeStruct(query.shape, BF16)],
        scratch_shapes=[
            pltpu.VMEM((DEVICES * ROWS, DH), F32),
            pltpu.VMEM((PER, DEVICES, DH), F32),
            pltpu.SemaphoreType.DMA,
        ],
        compiler_params=pltpu.CompilerParams(vmem_limit_bytes=16 << 20),
        name="block_scan",
    )(block, moved, pltpu.with_memory_space_constraint(decayed, pltpu.HBM))

    entering = exchange(states)

    return pl.pallas_call(
        finish_kernel,
        in_specs=[vmem] * 4,
        out_specs=pl.BlockSpec(memory_space=pl.ANY),
        out_shape=jax.ShapeDtypeStruct(query.shape, BF16),
        scratch_shapes=[pltpu.VMEM(query.shape, BF16), pltpu.SemaphoreType.DMA((GROUPS,))],
        compiler_params=pltpu.CompilerParams(vmem_limit_bytes=16 << 20),
        name="finish",
    )(decayed, entering, within, gain)


def solution(mesh):
    placed = P(("seq", "head"), None)
    return jax.shard_map(
        body, mesh=mesh, in_specs=(placed, placed, placed, placed, P(), P()), out_specs=placed, check_vma=False
    )
```

```python
import jax
import jax.numpy as jnp
from jax import lax
from jax.experimental import pallas as pl
from jax.experimental.pallas import tpu as pltpu
from jax.sharding import PartitionSpec as P

BLOCK = 256
DH = 128
HEADS = 40
GROUPS = 8
PER = HEADS // GROUPS
SLABS = 16
DEVICES = GROUPS * SLABS
STEP_GROUPS = 4
ROWS = PER * 8 + 2
F32 = jnp.float32
BF16 = jnp.bfloat16
VMEM = 58 << 20


def doc_row(docs_ref, block):
    rows = docs_ref[pl.ds(2 * block, 2), :]
    row = jnp.concatenate([rows[0:1], rows[1:2]], axis=1)
    before = docs_ref[pl.ds(jnp.maximum(2 * block - 1, 0), 1), :]
    prev = jnp.where(block == 0, row[:, 0:1], before[:, DH - 1 : DH])
    return row, prev


def lower_ones():
    t = lax.broadcasted_iota(jnp.int32, (BLOCK, BLOCK), 0)
    s = lax.broadcasted_iota(jnp.int32, (BLOCK, BLOCK), 1)
    return t >= s


def cum_rows(decay):
    tri = lower_ones().astype(F32).astype(BF16)
    return lax.dot_general(decay, tri, (((1,), (1,)), ((), ())), preferred_element_type=F32)


def state_kernel(block_ref, key_ref, value_ref, decay_ref, docs_ref, out_ref, scale_ref, wide_ref):
    step = pl.program_id(0)

    @pl.when(step == 0)
    def _():
        row, prev = doc_row(docs_ref, block_ref[0])
        last = row[:, BLOCK - 1 : BLOCK]
        decay = decay_ref[...]
        cum = cum_rows(decay)
        final = cum[:, BLOCK - 1 : BLOCK]
        same = (row == last).astype(F32)
        scale_ref[...] = jnp.exp(final - cum) * same
        ones = jnp.ones((8, BLOCK), BF16)
        final = lax.dot_general(ones, decay, (((1,), (1,)), ((), ())), preferred_element_type=F32)
        factor = jnp.exp(final) * (last == prev).astype(F32)
        high = factor.astype(BF16).astype(F32)
        middle = (factor - high).astype(BF16).astype(F32)
        low = factor - high - middle
        parts = jnp.concatenate([high, middle, low, jnp.zeros((8, DH - 3 * HEADS), F32)], axis=1)
        for piece in range(STEP_GROUPS * SLABS):
            wide_ref[(piece + 1) * ROWS - 2 : (piece + 1) * ROWS, :] = parts[0:2]

    for sub in range(STEP_GROUPS):
        first = (step * STEP_GROUPS + sub) * PER
        start = sub * SLABS * ROWS
        for one in range(PER):
            cols = slice((sub * PER + one) * DH, (sub * PER + one + 1) * DH)
            keys = key_ref[:, cols].T.astype(F32)
            decayed = (keys * scale_ref[pl.ds(first + one, 1), :]).astype(BF16)
            update = jnp.dot(decayed, value_ref[:, cols], preferred_element_type=F32)
            for slab in range(SLABS):
                at = start + slab * ROWS + one * 8
                wide_ref[at : at + 8, :] = update[slab * 8 : (slab + 1) * 8]
        rows = slice(start, start + SLABS * ROWS)
        out_ref[rows, :] = wide_ref[rows, :].astype(BF16)


def scan_kernel(block_ref, update_ref, decayed_hbm, out_ref, decayed_ref, wide_ref, factor_ref, sem):
    fetch = pltpu.make_async_copy(decayed_hbm, decayed_ref, sem)
    fetch.start()
    row = lax.broadcasted_iota(jnp.int32, (DH, PER * DH), 0)
    column = lax.broadcasted_iota(jnp.int32, (DH, PER * DH), 1)
    head = (block_ref[0] // SLABS) * PER + column // DH
    pick = (row == head) | (row == head + HEADS) | (row == head + 2 * HEADS)
    pick = pick.astype(F32).astype(BF16)
    for g in range(GROUPS):
        first = g * SLABS * ROWS
        rows = slice(first, first + SLABS * ROWS)
        wide_ref[rows, :] = update_ref[rows, :].astype(F32)
        parts = wide_ref[pl.ds(first + ROWS - 2, SLABS, stride=ROWS), :].astype(BF16)
        factor_ref[g * SLABS : (g + 1) * SLABS, :] = jnp.dot(parts, pick, preferred_element_type=F32)
    state = [jnp.zeros((8, DH), F32) for _ in range(PER)]
    for b in range(DEVICES):
        for one in range(PER):
            at = b * ROWS + one * 8
            out_ref[b, one] = state[one].astype(BF16)
            factor = factor_ref[b : b + 1, one * DH : (one + 1) * DH]
            state[one] = factor * state[one] + wide_ref[at : at + 8, :]
    fetch.wait()


def local_kernel(
    block_ref, query_ref, key_ref, value_ref, decay_ref, docs_ref, within_ref, decayed_ref, row_ref, col_ref, use_ref, mask_ref
):
    group = pl.program_id(0)

    @pl.when(group == 0)
    def _():
        row, prev = doc_row(docs_ref, block_ref[0])
        decay = decay_ref[...]
        row_ref[...] = cum_rows(decay)
        lower = lower_ones()
        ones = lower.astype(F32).astype(BF16)
        cum = lax.dot_general(ones, decay, (((1,), (1,)), ((), ())), preferred_element_type=F32)
        rows = jnp.broadcast_to(row.astype(F32), (BLOCK, BLOCK))
        cols = rows.T
        mask_ref[...] = (lower & (rows == cols)).astype(F32)
        usable = (cols[:, 0:1] == prev.astype(F32)).astype(F32)
        use = jnp.exp(cum) * usable
        for g in range(GROUPS):
            col_ref[g] = cum[:, g * PER : (g + 1) * PER]
            use_ref[g] = use[:, g * PER : (g + 1) * PER]

    allowed = mask_ref[...] > 0.5
    for one in range(PER):
        cols = slice(one * DH, (one + 1) * DH)
        query = query_ref[:, cols]
        scores = lax.dot_general(query, key_ref[:, cols], (((1,), (1,)), ((), ())), preferred_element_type=F32)
        exponent = col_ref[group, :, one : one + 1] - row_ref[pl.ds(group * PER + one, 1), :]
        mask = jnp.exp(jnp.where(allowed, exponent, -jnp.inf))
        weights = (scores * mask).astype(BF16)
        within_ref[:, cols] = jnp.dot(weights, value_ref[:, cols], preferred_element_type=F32)
        decayed_ref[:, cols] = (query.astype(F32) * use_ref[group, :, one : one + 1]).astype(BF16)


def finish_kernel(decayed_ref, state_ref, within_ref, gain_ref, out_hbm, out_ref, sems):
    copies = []
    for g in range(GROUPS):
        for one in range(g * PER, (g + 1) * PER):
            cols = slice(one * DH, (one + 1) * DH)
            state = state_ref[g * SLABS : (g + 1) * SLABS, one - g * PER].reshape(DH, DH)
            carried = jnp.dot(decayed_ref[:, cols], state, preferred_element_type=F32)
            total = within_ref[:, cols] + carried
            square = jnp.mean(total * total, axis=1, keepdims=True)
            out_ref[:, cols] = (total * lax.rsqrt(square + 1e-05) * gain_ref[:, cols]).astype(BF16)
        cols = slice(g * PER * DH, (g + 1) * PER * DH)
        copies.append(pltpu.make_async_copy(out_ref.at[:, cols], out_hbm.at[:, cols], sems.at[g]))
        copies[-1].start()
    for copy in copies:
        copy.wait()


def body(query, keyed, valued, decay, documents, gain):
    axes = ("seq", "head")
    block = lax.axis_index(axes).astype(jnp.int32).reshape(1)
    docs = documents.reshape(-1, DH)
    gain = gain.reshape(1, -1)
    decay = decay.T
    wide = PER * DH
    rows = pl.BlockSpec((BLOCK, wide), lambda g, *_: (0, g))
    whole = lambda a: pl.BlockSpec(a.shape, lambda g, *_: (0,) * a.ndim)

    wider = pl.BlockSpec((BLOCK, STEP_GROUPS * wide), lambda g, *_: (0, g))
    step_rows = STEP_GROUPS * SLABS * ROWS
    update = pl.pallas_call(
        state_kernel,
        grid_spec=pltpu.PrefetchScalarGridSpec(
            num_scalar_prefetch=1,
            grid=(GROUPS // STEP_GROUPS,),
            in_specs=[wider, wider, whole(decay), whole(docs)],
            out_specs=pl.BlockSpec((step_rows, DH), lambda g, *_: (g, 0)),
            scratch_shapes=[pltpu.VMEM((HEADS, BLOCK), F32), pltpu.VMEM((step_rows, DH), F32)],
        ),
        out_shape=jax.ShapeDtypeStruct((DEVICES * ROWS, DH), BF16),
        compiler_params=pltpu.CompilerParams(vmem_limit_bytes=VMEM),
        cost_estimate=pl.CostEstimate(flops=340_000_000, bytes_accessed=7_000_000, transcendentals=10_000),
        name="state_update",
    )(block, keyed, valued, decay, docs)

    def exchange(pieces):
        return lax.all_to_all(pieces, axes, split_axis=0, concat_axis=0, tiled=True)

    moved = exchange(update.reshape(DEVICES, ROWS // 2, 2, DH)).reshape(DEVICES * ROWS, DH)

    within, decayed = pl.pallas_call(
        local_kernel,
        grid_spec=pltpu.PrefetchScalarGridSpec(
            num_scalar_prefetch=1,
            grid=(GROUPS,),
            in_specs=[rows, rows, rows, whole(decay), whole(docs)],
            out_specs=[rows, rows],
            scratch_shapes=[
                pltpu.VMEM((HEADS, BLOCK), F32),
                pltpu.VMEM((GROUPS, BLOCK, PER), F32),
                pltpu.VMEM((GROUPS, BLOCK, PER), F32),
                pltpu.VMEM((BLOCK, BLOCK), F32),
            ],
        ),
        out_shape=[jax.ShapeDtypeStruct(query.shape, F32), jax.ShapeDtypeStruct(query.shape, BF16)],
        compiler_params=pltpu.CompilerParams(vmem_limit_bytes=VMEM),
        cost_estimate=pl.CostEstimate(flops=1_400_000_000, bytes_accessed=16_000_000, transcendentals=2_700_000),
        name="local_attention",
    )(block, query, keyed, valued, decay, docs)

    moved, within, decayed = lax.optimization_barrier((moved, within, decayed))
    vmem = pl.BlockSpec(memory_space=pltpu.VMEM)
    states, decayed = pl.pallas_call(
        scan_kernel,
        in_specs=[pl.BlockSpec(memory_space=pltpu.SMEM), vmem, pl.BlockSpec(memory_space=pltpu.HBM)],
        out_specs=[vmem, vmem],
        out_shape=[jax.ShapeDtypeStruct((DEVICES, PER, 8, DH), BF16), jax.ShapeDtypeStruct(query.shape, BF16)],
        scratch_shapes=[
            pltpu.VMEM((DEVICES * ROWS, DH), F32),
            pltpu.VMEM((DEVICES, PER * DH), F32),
            pltpu.SemaphoreType.DMA,
        ],
        compiler_params=pltpu.CompilerParams(vmem_limit_bytes=16 << 20),
        name="block_scan",
    )(block, moved, pltpu.with_memory_space_constraint(decayed, pltpu.HBM))

    entering = exchange(states)

    return pl.pallas_call(
        finish_kernel,
        in_specs=[vmem] * 4,
        out_specs=pl.BlockSpec(memory_space=pl.ANY),
        out_shape=jax.ShapeDtypeStruct(query.shape, BF16),
        scratch_shapes=[pltpu.VMEM(query.shape, BF16), pltpu.SemaphoreType.DMA((GROUPS,))],
        compiler_params=pltpu.CompilerParams(vmem_limit_bytes=16 << 20),
        name="finish",
    )(decayed, entering, within, gain)


def solution(mesh):
    placed = P(("seq", "head"), None)
    return jax.shard_map(
        body, mesh=mesh, in_specs=(placed, placed, placed, placed, P(), P()), out_specs=placed, check_vma=False
    )
```

```python
import jax
import jax.numpy as jnp
from jax import lax
from jax.experimental import pallas as pl
from jax.experimental.pallas import tpu as pltpu
from jax.sharding import PartitionSpec as P

BLOCK = 256
DH = 128
HEADS = 40
GROUPS = 8
PER = HEADS // GROUPS
SLABS = 16
DEVICES = GROUPS * SLABS
STEP_GROUPS = 4
ROWS = PER * 8 + 2


def member_order():
    order = []
    for i in range(DEVICES):
        bit = [(i >> k) & 1 for k in range(7)]
        x, y, z = (bit[k] + 2 * bit[k + 4] for k in range(3))
        order.append(((y * 4 + z) * 2 + bit[3]) * 4 + x)
    return order


ORDER = member_order()
F32 = jnp.float32
BF16 = jnp.bfloat16
VMEM = 58 << 20


def doc_row(docs_ref, block):
    rows = docs_ref[pl.ds(2 * block, 2), :]
    row = jnp.concatenate([rows[0:1], rows[1:2]], axis=1)
    before = docs_ref[pl.ds(jnp.maximum(2 * block - 1, 0), 1), :]
    prev = jnp.where(block == 0, row[:, 0:1], before[:, DH - 1 : DH])
    return row, prev


def lower_ones():
    t = lax.broadcasted_iota(jnp.int32, (BLOCK, BLOCK), 0)
    s = lax.broadcasted_iota(jnp.int32, (BLOCK, BLOCK), 1)
    return t >= s


def cum_rows(decay):
    tri = lower_ones().astype(F32).astype(BF16)
    return lax.dot_general(decay, tri, (((1,), (1,)), ((), ())), preferred_element_type=F32)


def state_kernel(block_ref, key_ref, value_ref, decay_ref, docs_ref, out_hbm, scale_ref, wide_ref, out_ref, sems):
    step = pl.program_id(0)
    pair = 2 * SLABS * ROWS

    @pl.when(step == 0)
    def _():
        row, prev = doc_row(docs_ref, block_ref[0])
        last = row[:, BLOCK - 1 : BLOCK]
        decay = decay_ref[...]
        cum = cum_rows(decay)
        final = cum[:, BLOCK - 1 : BLOCK]
        same = (row == last).astype(F32)
        scale_ref[...] = jnp.exp(final - cum) * same
        ones = jnp.ones((8, BLOCK), BF16)
        final = lax.dot_general(ones, decay, (((1,), (1,)), ((), ())), preferred_element_type=F32)
        factor = jnp.exp(final) * (last == prev).astype(F32)
        high = factor.astype(BF16).astype(F32)
        middle = (factor - high).astype(BF16).astype(F32)
        low = factor - high - middle
        parts = jnp.concatenate([high, middle, low, jnp.zeros((8, DH - 3 * HEADS), F32)], axis=1)
        for piece in range(STEP_GROUPS * SLABS):
            wide_ref[(piece + 1) * ROWS - 2 : (piece + 1) * ROWS, :] = parts[0:2]

    for sub in range(STEP_GROUPS):
        first = (step * STEP_GROUPS + sub) * PER
        start = sub * SLABS * ROWS
        for one in range(PER):
            cols = slice((sub * PER + one) * DH, (sub * PER + one + 1) * DH)
            keys = key_ref[:, cols].T.astype(F32)
            decayed = (keys * scale_ref[pl.ds(first + one, 1), :]).astype(BF16)
            update = jnp.dot(decayed, value_ref[:, cols], preferred_element_type=F32)
            for slab in range(SLABS):
                at = start + slab * ROWS + one * 8
                wide_ref[at : at + 8, :] = update[slab * 8 : (slab + 1) * 8]
        rows = slice(start, start + SLABS * ROWS)
        at = step * (STEP_GROUPS * SLABS * ROWS) + start
        out_ref[pl.ds(at, SLABS * ROWS), :] = wide_ref[rows, :].astype(BF16)
        if sub % 2 == 1:
            done = pl.ds(at - SLABS * ROWS, pair)
            number = step * (STEP_GROUPS // 2) + sub // 2
            pltpu.make_async_copy(out_ref.at[done], out_hbm.at[done], sems.at[number]).start()

    @pl.when(step == GROUPS // STEP_GROUPS - 1)
    def _():
        for number in range(GROUPS // 2):
            done = slice(number * pair, (number + 1) * pair)
            pltpu.make_async_copy(out_ref.at[done], out_hbm.at[done], sems.at[number]).wait()


def scan_kernel(block_ref, update_ref, decayed_hbm, out_ref, decayed_ref, wide_ref, factor_ref, sem):
    fetch = pltpu.make_async_copy(decayed_hbm, decayed_ref, sem)
    fetch.start()
    block = block_ref[0]
    group = ((block >> 1) & 1) + 2 * ((block >> 6) & 1) + 4 * ((block >> 4) & 1)
    row = lax.broadcasted_iota(jnp.int32, (DH, PER * DH), 0)
    column = lax.broadcasted_iota(jnp.int32, (DH, PER * DH), 1)
    head = group * PER + (column >> 7)
    pick = (row == head) | (row == head + HEADS) | (row == head + 2 * HEADS)
    pick = pick.astype(F32).astype(BF16)
    for g in range(GROUPS):
        first = g * SLABS * ROWS
        rows = slice(first, first + SLABS * ROWS)
        wide_ref[rows, :] = update_ref[rows, :].astype(F32)
        parts = wide_ref[pl.ds(first + ROWS - 2, SLABS, stride=ROWS), :].astype(BF16)
        factor_ref[g * SLABS : (g + 1) * SLABS, :] = jnp.dot(parts, pick, preferred_element_type=F32)
    state = [jnp.zeros((8, DH), F32) for _ in range(PER)]
    for b in range(DEVICES):
        place = ORDER.index(b)
        for one in range(PER):
            at = place * ROWS + one * 8
            out_ref[place, one] = state[one].astype(BF16)
            factor = factor_ref[place : place + 1, one * DH : (one + 1) * DH]
            state[one] = factor * state[one] + wide_ref[at : at + 8, :]
    fetch.wait()


def local_kernel(
    block_ref, query_ref, key_ref, value_ref, decay_ref, docs_ref, within_ref, decayed_ref, row_ref, col_ref, use_ref, mask_ref
):
    group = pl.program_id(0)

    @pl.when(group == 0)
    def _():
        row, prev = doc_row(docs_ref, block_ref[0])
        decay = decay_ref[...]
        row_ref[...] = cum_rows(decay)
        lower = lower_ones()
        ones = lower.astype(F32).astype(BF16)
        cum = lax.dot_general(ones, decay, (((1,), (1,)), ((), ())), preferred_element_type=F32)
        rows = jnp.broadcast_to(row.astype(F32), (BLOCK, BLOCK))
        cols = rows.T
        mask_ref[...] = (lower & (rows == cols)).astype(F32)
        usable = (cols[:, 0:1] == prev.astype(F32)).astype(F32)
        use = jnp.exp(cum) * usable
        for g in range(GROUPS):
            col_ref[g] = cum[:, g * PER : (g + 1) * PER]
            use_ref[g] = use[:, g * PER : (g + 1) * PER]

    allowed = mask_ref[...] > 0.5
    for one in range(PER):
        cols = slice(one * DH, (one + 1) * DH)
        query = query_ref[:, cols]
        scores = lax.dot_general(query, key_ref[:, cols], (((1,), (1,)), ((), ())), preferred_element_type=F32)
        exponent = col_ref[group, :, one : one + 1] - row_ref[pl.ds(group * PER + one, 1), :]
        mask = jnp.exp(jnp.where(allowed, exponent, -jnp.inf))
        weights = (scores * mask).astype(BF16)
        within_ref[:, cols] = jnp.dot(weights, value_ref[:, cols], preferred_element_type=F32)
        decayed_ref[:, cols] = (query.astype(F32) * use_ref[group, :, one : one + 1]).astype(BF16)


def finish_kernel(decayed_ref, state_ref, within_ref, gain_ref, out_hbm, out_ref, sems):
    copies = []
    for g in range(GROUPS):
        for one in range(g * PER, (g + 1) * PER):
            cols = slice(one * DH, (one + 1) * DH)
            state = state_ref[g * SLABS : (g + 1) * SLABS, one - g * PER].reshape(DH, DH)
            carried = jnp.dot(decayed_ref[:, cols], state, preferred_element_type=F32)
            total = within_ref[:, cols] + carried
            square = jnp.mean(total * total, axis=1, keepdims=True)
            out_ref[:, cols] = (total * lax.rsqrt(square + 1e-05) * gain_ref[:, cols]).astype(BF16)
        cols = slice(g * PER * DH, (g + 1) * PER * DH)
        copies.append(pltpu.make_async_copy(out_ref.at[:, cols], out_hbm.at[:, cols], sems.at[g]))
        copies[-1].start()
    for copy in copies:
        copy.wait()


def body(query, keyed, valued, decay, documents, gain):
    axes = ("seq", "head")
    block = lax.axis_index(axes).astype(jnp.int32).reshape(1)
    docs = documents.reshape(-1, DH)
    gain = gain.reshape(1, -1)
    decay = decay.T
    wide = PER * DH
    rows = pl.BlockSpec((BLOCK, wide), lambda g, *_: (0, g))
    whole = lambda a: pl.BlockSpec(a.shape, lambda g, *_: (0,) * a.ndim)

    wider = pl.BlockSpec((BLOCK, STEP_GROUPS * wide), lambda g, *_: (0, g))
    step_rows = STEP_GROUPS * SLABS * ROWS
    update = pl.pallas_call(
        state_kernel,
        grid_spec=pltpu.PrefetchScalarGridSpec(
            num_scalar_prefetch=1,
            grid=(GROUPS // STEP_GROUPS,),
            in_specs=[wider, wider, whole(decay), whole(docs)],
            out_specs=pl.BlockSpec(memory_space=pl.ANY),
            scratch_shapes=[
                pltpu.VMEM((HEADS, BLOCK), F32),
                pltpu.VMEM((step_rows, DH), F32),
                pltpu.VMEM((DEVICES * ROWS, DH), BF16),
                pltpu.SemaphoreType.DMA((GROUPS // 2,)),
            ],
        ),
        out_shape=jax.ShapeDtypeStruct((DEVICES * ROWS, DH), BF16),
        compiler_params=pltpu.CompilerParams(vmem_limit_bytes=VMEM),
        cost_estimate=pl.CostEstimate(flops=340_000_000, bytes_accessed=7_000_000, transcendentals=10_000),
        name="state_update",
    )(block, keyed, valued, decay, docs)

    def exchange(pieces):
        return lax.all_to_all(
            pieces, axes, split_axis=0, concat_axis=0, axis_index_groups=[ORDER], tiled=True
        )

    moved = exchange(update.reshape(DEVICES, ROWS // 2, 2, DH)).reshape(DEVICES * ROWS, DH)

    within, decayed = pl.pallas_call(
        local_kernel,
        grid_spec=pltpu.PrefetchScalarGridSpec(
            num_scalar_prefetch=1,
            grid=(GROUPS,),
            in_specs=[rows, rows, rows, whole(decay), whole(docs)],
            out_specs=[rows, rows],
            scratch_shapes=[
                pltpu.VMEM((HEADS, BLOCK), F32),
                pltpu.VMEM((GROUPS, BLOCK, PER), F32),
                pltpu.VMEM((GROUPS, BLOCK, PER), F32),
                pltpu.VMEM((BLOCK, BLOCK), F32),
            ],
        ),
        out_shape=[jax.ShapeDtypeStruct(query.shape, F32), jax.ShapeDtypeStruct(query.shape, BF16)],
        compiler_params=pltpu.CompilerParams(vmem_limit_bytes=VMEM),
        cost_estimate=pl.CostEstimate(flops=1_400_000_000, bytes_accessed=16_000_000, transcendentals=2_700_000),
        name="local_attention",
    )(block, query, keyed, valued, decay, docs)

    moved, within, decayed = lax.optimization_barrier((moved, within, decayed))
    vmem = pl.BlockSpec(memory_space=pltpu.VMEM)
    states, decayed = pl.pallas_call(
        scan_kernel,
        in_specs=[pl.BlockSpec(memory_space=pltpu.SMEM), vmem, pl.BlockSpec(memory_space=pltpu.HBM)],
        out_specs=[vmem, vmem],
        out_shape=[jax.ShapeDtypeStruct((DEVICES, PER, 8, DH), BF16), jax.ShapeDtypeStruct(query.shape, BF16)],
        scratch_shapes=[
            pltpu.VMEM((DEVICES * ROWS, DH), F32),
            pltpu.VMEM((DEVICES, PER * DH), F32),
            pltpu.SemaphoreType.DMA,
        ],
        compiler_params=pltpu.CompilerParams(vmem_limit_bytes=16 << 20),
        name="block_scan",
    )(block, moved, pltpu.with_memory_space_constraint(decayed, pltpu.HBM))

    entering = exchange(states)

    return pl.pallas_call(
        finish_kernel,
        in_specs=[vmem] * 4,
        out_specs=pl.BlockSpec(memory_space=pl.ANY),
        out_shape=jax.ShapeDtypeStruct(query.shape, BF16),
        scratch_shapes=[pltpu.VMEM(query.shape, BF16), pltpu.SemaphoreType.DMA((GROUPS,))],
        compiler_params=pltpu.CompilerParams(vmem_limit_bytes=16 << 20),
        name="finish",
    )(decayed, entering, within, gain)


def solution(mesh):
    placed = P(("seq", "head"), None)
    return jax.shard_map(
        body, mesh=mesh, in_specs=(placed, placed, placed, placed, P(), P()), out_specs=placed, check_vma=False
    )
```

```python
import jax
import jax.numpy as jnp
from jax import lax
from jax.experimental import pallas as pl
from jax.experimental.pallas import tpu as pltpu
from jax.sharding import PartitionSpec as P

BLOCK = 256
DH = 128
HEADS = 40
GROUPS = 8
PER = HEADS // GROUPS
SLABS = 16
DEVICES = GROUPS * SLABS
STEP_GROUPS = 4
ROWS = PER * 8 + 2


def member_order():
    order = []
    for i in range(DEVICES):
        bit = [(i >> k) & 1 for k in range(7)]
        x, y, z = (bit[k] + 2 * bit[k + 4] for k in range(3))
        order.append(((y * 4 + z) * 2 + bit[3]) * 4 + x)
    return order


ORDER = member_order()
F32 = jnp.float32
BF16 = jnp.bfloat16
VMEM = 58 << 20


def doc_row(docs_ref, block):
    rows = docs_ref[pl.ds(2 * block, 2), :]
    row = jnp.concatenate([rows[0:1], rows[1:2]], axis=1)
    before = docs_ref[pl.ds(jnp.maximum(2 * block - 1, 0), 1), :]
    prev = jnp.where(block == 0, row[:, 0:1], before[:, DH - 1 : DH])
    return row, prev


def lower_ones():
    t = lax.broadcasted_iota(jnp.int32, (BLOCK, BLOCK), 0)
    s = lax.broadcasted_iota(jnp.int32, (BLOCK, BLOCK), 1)
    return t >= s


def cum_rows(decay):
    tri = lower_ones().astype(F32).astype(BF16)
    return lax.dot_general(decay, tri, (((1,), (1,)), ((), ())), preferred_element_type=F32)


def state_kernel(block_ref, key_ref, value_ref, decay_ref, docs_ref, out_hbm, scale_ref, wide_ref, out_ref, sems):
    step = pl.program_id(0)
    pair = 2 * SLABS * ROWS

    @pl.when(step == 0)
    def _():
        row, prev = doc_row(docs_ref, block_ref[0])
        last = row[:, BLOCK - 1 : BLOCK]
        decay = decay_ref[...]
        cum = cum_rows(decay)
        final = cum[:, BLOCK - 1 : BLOCK]
        same = (row == last).astype(F32)
        scale_ref[...] = jnp.exp(final - cum) * same
        ones = jnp.ones((8, BLOCK), BF16)
        final = lax.dot_general(ones, decay, (((1,), (1,)), ((), ())), preferred_element_type=F32)
        factor = jnp.exp(final) * (last == prev).astype(F32)
        high = factor.astype(BF16).astype(F32)
        middle = (factor - high).astype(BF16).astype(F32)
        low = factor - high - middle
        parts = jnp.concatenate([high, middle, low, jnp.zeros((8, DH - 3 * HEADS), F32)], axis=1)
        for piece in range(STEP_GROUPS * SLABS):
            wide_ref[(piece + 1) * ROWS - 2 : (piece + 1) * ROWS, :] = parts[0:2]

    for sub in range(STEP_GROUPS):
        first = (step * STEP_GROUPS + sub) * PER
        start = sub * SLABS * ROWS
        for one in range(PER):
            cols = slice((sub * PER + one) * DH, (sub * PER + one + 1) * DH)
            keys = key_ref[:, cols].T.astype(F32)
            decayed = (keys * scale_ref[pl.ds(first + one, 1), :]).astype(BF16)
            update = jnp.dot(decayed, value_ref[:, cols], preferred_element_type=F32)
            for slab in range(SLABS):
                at = start + slab * ROWS + one * 8
                wide_ref[at : at + 8, :] = update[slab * 8 : (slab + 1) * 8]
        rows = slice(start, start + SLABS * ROWS)
        at = step * (STEP_GROUPS * SLABS * ROWS) + start
        out_ref[pl.ds(at, SLABS * ROWS), :] = wide_ref[rows, :].astype(BF16)
        if sub % 2 == 1:
            done = pl.ds(at - SLABS * ROWS, pair)
            number = step * (STEP_GROUPS // 2) + sub // 2
            pltpu.make_async_copy(out_ref.at[done], out_hbm.at[done], sems.at[number]).start()

    @pl.when(step == GROUPS // STEP_GROUPS - 1)
    def _():
        for number in range(GROUPS // 2):
            done = slice(number * pair, (number + 1) * pair)
            pltpu.make_async_copy(out_ref.at[done], out_hbm.at[done], sems.at[number]).wait()


def scan_kernel(block_ref, update_ref, decayed_hbm, out_ref, decayed_ref, wide_ref, factor_ref, sem):
    fetch = pltpu.make_async_copy(decayed_hbm, decayed_ref, sem)
    fetch.start()
    block = block_ref[0]
    group = ((block >> 1) & 1) + 2 * ((block >> 6) & 1) + 4 * ((block >> 4) & 1)
    row = lax.broadcasted_iota(jnp.int32, (DH, PER * DH), 0)
    column = lax.broadcasted_iota(jnp.int32, (DH, PER * DH), 1)
    head = group * PER + (column >> 7)
    pick = (row == head) | (row == head + HEADS) | (row == head + 2 * HEADS)
    pick = pick.astype(F32).astype(BF16)
    for g in range(GROUPS):
        first = g * SLABS * ROWS
        rows = slice(first, first + SLABS * ROWS)
        wide_ref[rows, :] = update_ref[rows, :].astype(F32)
        parts = wide_ref[pl.ds(first + ROWS - 2, SLABS, stride=ROWS), :].astype(BF16)
        factor_ref[g * SLABS : (g + 1) * SLABS, :] = jnp.dot(parts, pick, preferred_element_type=F32)
    state = [jnp.zeros((8, DH), F32) for _ in range(PER)]
    for b in range(DEVICES):
        place = ORDER.index(b)
        for one in range(PER):
            at = place * ROWS + one * 8
            out_ref[b, one] = state[one].astype(BF16)
            factor = factor_ref[place : place + 1, one * DH : (one + 1) * DH]
            state[one] = factor * state[one] + wide_ref[at : at + 8, :]
    fetch.wait()


def local_kernel(
    block_ref, query_ref, key_ref, value_ref, decay_ref, docs_ref, within_ref, decayed_ref, row_ref, col_ref, use_ref, mask_ref
):
    group = pl.program_id(0)

    @pl.when(group == 0)
    def _():
        row, prev = doc_row(docs_ref, block_ref[0])
        decay = decay_ref[...]
        row_ref[...] = cum_rows(decay)
        lower = lower_ones()
        ones = lower.astype(F32).astype(BF16)
        cum = lax.dot_general(ones, decay, (((1,), (1,)), ((), ())), preferred_element_type=F32)
        rows = jnp.broadcast_to(row.astype(F32), (BLOCK, BLOCK))
        cols = rows.T
        mask_ref[...] = (lower & (rows == cols)).astype(F32)
        usable = (cols[:, 0:1] == prev.astype(F32)).astype(F32)
        use = jnp.exp(cum) * usable
        for g in range(GROUPS):
            col_ref[g] = cum[:, g * PER : (g + 1) * PER]
            use_ref[g] = use[:, g * PER : (g + 1) * PER]

    allowed = mask_ref[...] > 0.5
    for one in range(PER):
        cols = slice(one * DH, (one + 1) * DH)
        query = query_ref[:, cols]
        scores = lax.dot_general(query, key_ref[:, cols], (((1,), (1,)), ((), ())), preferred_element_type=F32)
        exponent = col_ref[group, :, one : one + 1] - row_ref[pl.ds(group * PER + one, 1), :]
        mask = jnp.exp(jnp.where(allowed, exponent, -jnp.inf))
        weights = (scores * mask).astype(BF16)
        within_ref[:, cols] = jnp.dot(weights, value_ref[:, cols], preferred_element_type=F32)
        decayed_ref[:, cols] = (query.astype(F32) * use_ref[group, :, one : one + 1]).astype(BF16)


def finish_kernel(decayed_ref, state_ref, within_ref, gain_ref, out_hbm, out_ref, sems):
    copies = []
    for g in range(GROUPS):
        for one in range(g * PER, (g + 1) * PER):
            cols = slice(one * DH, (one + 1) * DH)
            slabs = [state_ref[ORDER[g * SLABS + slab], one - g * PER] for slab in range(SLABS)]
            state = jnp.stack(slabs).reshape(DH, DH)
            carried = jnp.dot(decayed_ref[:, cols], state, preferred_element_type=F32)
            total = within_ref[:, cols] + carried
            square = jnp.mean(total * total, axis=1, keepdims=True)
            out_ref[:, cols] = (total * lax.rsqrt(square + 1e-05) * gain_ref[:, cols]).astype(BF16)
        cols = slice(g * PER * DH, (g + 1) * PER * DH)
        copies.append(pltpu.make_async_copy(out_ref.at[:, cols], out_hbm.at[:, cols], sems.at[g]))
        copies[-1].start()
    for copy in copies:
        copy.wait()


def body(query, keyed, valued, decay, documents, gain):
    axes = ("seq", "head")
    block = lax.axis_index(axes).astype(jnp.int32).reshape(1)
    docs = documents.reshape(-1, DH)
    gain = gain.reshape(1, -1)
    decay = decay.T
    wide = PER * DH
    rows = pl.BlockSpec((BLOCK, wide), lambda g, *_: (0, g))
    whole = lambda a: pl.BlockSpec(a.shape, lambda g, *_: (0,) * a.ndim)

    wider = pl.BlockSpec((BLOCK, STEP_GROUPS * wide), lambda g, *_: (0, g))
    step_rows = STEP_GROUPS * SLABS * ROWS
    update = pl.pallas_call(
        state_kernel,
        grid_spec=pltpu.PrefetchScalarGridSpec(
            num_scalar_prefetch=1,
            grid=(GROUPS // STEP_GROUPS,),
            in_specs=[wider, wider, whole(decay), whole(docs)],
            out_specs=pl.BlockSpec(memory_space=pl.ANY),
            scratch_shapes=[
                pltpu.VMEM((HEADS, BLOCK), F32),
                pltpu.VMEM((step_rows, DH), F32),
                pltpu.VMEM((DEVICES * ROWS, DH), BF16),
                pltpu.SemaphoreType.DMA((GROUPS // 2,)),
            ],
        ),
        out_shape=jax.ShapeDtypeStruct((DEVICES * ROWS, DH), BF16),
        compiler_params=pltpu.CompilerParams(vmem_limit_bytes=VMEM),
        cost_estimate=pl.CostEstimate(flops=340_000_000, bytes_accessed=7_000_000, transcendentals=10_000),
        name="state_update",
    )(block, keyed, valued, decay, docs)

    def exchange(pieces, groups):
        return lax.all_to_all(
            pieces, axes, split_axis=0, concat_axis=0, axis_index_groups=groups, tiled=True
        )

    moved = exchange(update.reshape(DEVICES, ROWS // 2, 2, DH), [ORDER]).reshape(DEVICES * ROWS, DH)

    within, decayed = pl.pallas_call(
        local_kernel,
        grid_spec=pltpu.PrefetchScalarGridSpec(
            num_scalar_prefetch=1,
            grid=(GROUPS,),
            in_specs=[rows, rows, rows, whole(decay), whole(docs)],
            out_specs=[rows, rows],
            scratch_shapes=[
                pltpu.VMEM((HEADS, BLOCK), F32),
                pltpu.VMEM((GROUPS, BLOCK, PER), F32),
                pltpu.VMEM((GROUPS, BLOCK, PER), F32),
                pltpu.VMEM((BLOCK, BLOCK), F32),
            ],
        ),
        out_shape=[jax.ShapeDtypeStruct(query.shape, F32), jax.ShapeDtypeStruct(query.shape, BF16)],
        compiler_params=pltpu.CompilerParams(vmem_limit_bytes=VMEM),
        cost_estimate=pl.CostEstimate(flops=1_400_000_000, bytes_accessed=16_000_000, transcendentals=2_700_000),
        name="local_attention",
    )(block, query, keyed, valued, decay, docs)

    moved, within, decayed = lax.optimization_barrier((moved, within, decayed))
    vmem = pl.BlockSpec(memory_space=pltpu.VMEM)
    states, decayed = pl.pallas_call(
        scan_kernel,
        in_specs=[pl.BlockSpec(memory_space=pltpu.SMEM), vmem, pl.BlockSpec(memory_space=pltpu.HBM)],
        out_specs=[vmem, vmem],
        out_shape=[jax.ShapeDtypeStruct((DEVICES, PER, 8, DH), BF16), jax.ShapeDtypeStruct(query.shape, BF16)],
        scratch_shapes=[
            pltpu.VMEM((DEVICES * ROWS, DH), F32),
            pltpu.VMEM((DEVICES, PER * DH), F32),
            pltpu.SemaphoreType.DMA,
        ],
        compiler_params=pltpu.CompilerParams(vmem_limit_bytes=16 << 20),
        name="block_scan",
    )(block, moved, pltpu.with_memory_space_constraint(decayed, pltpu.HBM))

    entering = exchange(states, None)

    return pl.pallas_call(
        finish_kernel,
        in_specs=[vmem] * 4,
        out_specs=pl.BlockSpec(memory_space=pl.ANY),
        out_shape=jax.ShapeDtypeStruct(query.shape, BF16),
        scratch_shapes=[pltpu.VMEM(query.shape, BF16), pltpu.SemaphoreType.DMA((GROUPS,))],
        compiler_params=pltpu.CompilerParams(vmem_limit_bytes=16 << 20),
        name="finish",
    )(decayed, entering, within, gain)


def solution(mesh):
    placed = P(("seq", "head"), None)
    return jax.shard_map(
        body, mesh=mesh, in_specs=(placed, placed, placed, placed, P(), P()), out_specs=placed, check_vma=False
    )
```

```python
import jax
import jax.numpy as jnp
from jax import lax
from jax.experimental import pallas as pl
from jax.experimental.pallas import tpu as pltpu
from jax.sharding import PartitionSpec as P

BLOCK = 256
DH = 128
HEADS = 40
GROUPS = 8
PER = HEADS // GROUPS
SLABS = 16
DEVICES = GROUPS * SLABS
STEP_GROUPS = 4
ROWS = PER * 8 + 2


def member_order():
    order = []
    for i in range(DEVICES):
        bit = [(i >> k) & 1 for k in range(7)]
        x, y, z = (bit[k] + 2 * bit[k + 3] for k in range(3))
        order.append(((y * 4 + z) * 2 + bit[6]) * 4 + x)
    return order


ORDER = member_order()
F32 = jnp.float32
BF16 = jnp.bfloat16
VMEM = 58 << 20


def doc_row(docs_ref, block):
    rows = docs_ref[pl.ds(2 * block, 2), :]
    row = jnp.concatenate([rows[0:1], rows[1:2]], axis=1)
    before = docs_ref[pl.ds(jnp.maximum(2 * block - 1, 0), 1), :]
    prev = jnp.where(block == 0, row[:, 0:1], before[:, DH - 1 : DH])
    return row, prev


def lower_ones():
    t = lax.broadcasted_iota(jnp.int32, (BLOCK, BLOCK), 0)
    s = lax.broadcasted_iota(jnp.int32, (BLOCK, BLOCK), 1)
    return t >= s


def cum_rows(decay):
    tri = lower_ones().astype(F32).astype(BF16)
    return lax.dot_general(decay, tri, (((1,), (1,)), ((), ())), preferred_element_type=F32)


def state_kernel(block_ref, key_ref, value_ref, decay_ref, docs_ref, out_hbm, scale_ref, wide_ref, out_ref, sems):
    step = pl.program_id(0)
    pair = 2 * SLABS * ROWS

    @pl.when(step == 0)
    def _():
        row, prev = doc_row(docs_ref, block_ref[0])
        last = row[:, BLOCK - 1 : BLOCK]
        decay = decay_ref[...]
        cum = cum_rows(decay)
        final = cum[:, BLOCK - 1 : BLOCK]
        same = (row == last).astype(F32)
        scale_ref[...] = jnp.exp(final - cum) * same
        ones = jnp.ones((8, BLOCK), BF16)
        final = lax.dot_general(ones, decay, (((1,), (1,)), ((), ())), preferred_element_type=F32)
        factor = jnp.exp(final) * (last == prev).astype(F32)
        high = factor.astype(BF16).astype(F32)
        middle = (factor - high).astype(BF16).astype(F32)
        low = factor - high - middle
        parts = jnp.concatenate([high, middle, low, jnp.zeros((8, DH - 3 * HEADS), F32)], axis=1)
        for piece in range(STEP_GROUPS * SLABS):
            wide_ref[(piece + 1) * ROWS - 2 : (piece + 1) * ROWS, :] = parts[0:2]

    for sub in range(STEP_GROUPS):
        first = (step * STEP_GROUPS + sub) * PER
        start = sub * SLABS * ROWS
        for one in range(PER):
            cols = slice((sub * PER + one) * DH, (sub * PER + one + 1) * DH)
            keys = key_ref[:, cols].T.astype(F32)
            decayed = (keys * scale_ref[pl.ds(first + one, 1), :]).astype(BF16)
            update = jnp.dot(decayed, value_ref[:, cols], preferred_element_type=F32)
            for slab in range(SLABS):
                at = start + slab * ROWS + one * 8
                wide_ref[at : at + 8, :] = update[slab * 8 : (slab + 1) * 8]
        rows = slice(start, start + SLABS * ROWS)
        at = step * (STEP_GROUPS * SLABS * ROWS) + start
        out_ref[pl.ds(at, SLABS * ROWS), :] = wide_ref[rows, :].astype(BF16)
        if sub % 2 == 1:
            done = pl.ds(at - SLABS * ROWS, pair)
            number = step * (STEP_GROUPS // 2) + sub // 2
            pltpu.make_async_copy(out_ref.at[done], out_hbm.at[done], sems.at[number]).start()

    @pl.when(step == GROUPS // STEP_GROUPS - 1)
    def _():
        for number in range(GROUPS // 2):
            done = slice(number * pair, (number + 1) * pair)
            pltpu.make_async_copy(out_ref.at[done], out_hbm.at[done], sems.at[number]).wait()


def scan_kernel(block_ref, update_ref, decayed_hbm, out_ref, decayed_ref, wide_ref, factor_ref, sem):
    fetch = pltpu.make_async_copy(decayed_hbm, decayed_ref, sem)
    fetch.start()
    block = block_ref[0]
    group = ((block >> 6) & 1) + 2 * ((block >> 4) & 1) + 4 * ((block >> 2) & 1)
    row = lax.broadcasted_iota(jnp.int32, (DH, PER * DH), 0)
    column = lax.broadcasted_iota(jnp.int32, (DH, PER * DH), 1)
    head = group * PER + (column >> 7)
    pick = (row == head) | (row == head + HEADS) | (row == head + 2 * HEADS)
    pick = pick.astype(F32).astype(BF16)
    for g in range(GROUPS):
        first = g * SLABS * ROWS
        rows = slice(first, first + SLABS * ROWS)
        wide_ref[rows, :] = update_ref[rows, :].astype(F32)
        parts = wide_ref[pl.ds(first + ROWS - 2, SLABS, stride=ROWS), :].astype(BF16)
        factor_ref[g * SLABS : (g + 1) * SLABS, :] = jnp.dot(parts, pick, preferred_element_type=F32)
    state = [jnp.zeros((8, DH), F32) for _ in range(PER)]
    for b in range(DEVICES):
        place = ORDER.index(b)
        for one in range(PER):
            at = place * ROWS + one * 8
            out_ref[place, one] = state[one].astype(BF16)
            factor = factor_ref[place : place + 1, one * DH : (one + 1) * DH]
            state[one] = factor * state[one] + wide_ref[at : at + 8, :]
    fetch.wait()


def local_kernel(
    block_ref, query_ref, key_ref, value_ref, decay_ref, docs_ref, within_ref, decayed_ref, row_ref, col_ref, use_ref, mask_ref
):
    group = pl.program_id(0)

    @pl.when(group == 0)
    def _():
        row, prev = doc_row(docs_ref, block_ref[0])
        decay = decay_ref[...]
        row_ref[...] = cum_rows(decay)
        lower = lower_ones()
        ones = lower.astype(F32).astype(BF16)
        cum = lax.dot_general(ones, decay, (((1,), (1,)), ((), ())), preferred_element_type=F32)
        rows = jnp.broadcast_to(row.astype(F32), (BLOCK, BLOCK))
        cols = rows.T
        mask_ref[...] = (lower & (rows == cols)).astype(F32)
        usable = (cols[:, 0:1] == prev.astype(F32)).astype(F32)
        use = jnp.exp(cum) * usable
        for g in range(GROUPS):
            col_ref[g] = cum[:, g * PER : (g + 1) * PER]
            use_ref[g] = use[:, g * PER : (g + 1) * PER]

    allowed = mask_ref[...] > 0.5
    for one in range(PER):
        cols = slice(one * DH, (one + 1) * DH)
        query = query_ref[:, cols]
        scores = lax.dot_general(query, key_ref[:, cols], (((1,), (1,)), ((), ())), preferred_element_type=F32)
        exponent = col_ref[group, :, one : one + 1] - row_ref[pl.ds(group * PER + one, 1), :]
        mask = jnp.exp(jnp.where(allowed, exponent, -jnp.inf))
        weights = (scores * mask).astype(BF16)
        within_ref[:, cols] = jnp.dot(weights, value_ref[:, cols], preferred_element_type=F32)
        decayed_ref[:, cols] = (query.astype(F32) * use_ref[group, :, one : one + 1]).astype(BF16)


def finish_kernel(decayed_ref, state_ref, within_ref, gain_ref, out_hbm, out_ref, sems):
    copies = []
    for g in range(GROUPS):
        for one in range(g * PER, (g + 1) * PER):
            cols = slice(one * DH, (one + 1) * DH)
            state = state_ref[g * SLABS : (g + 1) * SLABS, one - g * PER].reshape(DH, DH)
            carried = jnp.dot(decayed_ref[:, cols], state, preferred_element_type=F32)
            total = within_ref[:, cols] + carried
            square = jnp.mean(total * total, axis=1, keepdims=True)
            out_ref[:, cols] = (total * lax.rsqrt(square + 1e-05) * gain_ref[:, cols]).astype(BF16)
        cols = slice(g * PER * DH, (g + 1) * PER * DH)
        copies.append(pltpu.make_async_copy(out_ref.at[:, cols], out_hbm.at[:, cols], sems.at[g]))
        copies[-1].start()
    for copy in copies:
        copy.wait()


def body(query, keyed, valued, decay, documents, gain):
    axes = ("seq", "head")
    block = lax.axis_index(axes).astype(jnp.int32).reshape(1)
    docs = documents.reshape(-1, DH)
    gain = gain.reshape(1, -1)
    decay = decay.T
    wide = PER * DH
    rows = pl.BlockSpec((BLOCK, wide), lambda g, *_: (0, g))
    whole = lambda a: pl.BlockSpec(a.shape, lambda g, *_: (0,) * a.ndim)

    wider = pl.BlockSpec((BLOCK, STEP_GROUPS * wide), lambda g, *_: (0, g))
    step_rows = STEP_GROUPS * SLABS * ROWS
    update = pl.pallas_call(
        state_kernel,
        grid_spec=pltpu.PrefetchScalarGridSpec(
            num_scalar_prefetch=1,
            grid=(GROUPS // STEP_GROUPS,),
            in_specs=[wider, wider, whole(decay), whole(docs)],
            out_specs=pl.BlockSpec(memory_space=pl.ANY),
            scratch_shapes=[
                pltpu.VMEM((HEADS, BLOCK), F32),
                pltpu.VMEM((step_rows, DH), F32),
                pltpu.VMEM((DEVICES * ROWS, DH), BF16),
                pltpu.SemaphoreType.DMA((GROUPS // 2,)),
            ],
        ),
        out_shape=jax.ShapeDtypeStruct((DEVICES * ROWS, DH), BF16),
        compiler_params=pltpu.CompilerParams(vmem_limit_bytes=VMEM),
        cost_estimate=pl.CostEstimate(flops=340_000_000, bytes_accessed=7_000_000, transcendentals=10_000),
        name="state_update",
    )(block, keyed, valued, decay, docs)

    def exchange(pieces):
        return lax.all_to_all(
            pieces, axes, split_axis=0, concat_axis=0, axis_index_groups=[ORDER], tiled=True
        )

    moved = exchange(update.reshape(DEVICES, ROWS // 2, 2, DH)).reshape(DEVICES * ROWS, DH)

    within, decayed = pl.pallas_call(
        local_kernel,
        grid_spec=pltpu.PrefetchScalarGridSpec(
            num_scalar_prefetch=1,
            grid=(GROUPS,),
            in_specs=[rows, rows, rows, whole(decay), whole(docs)],
            out_specs=[rows, rows],
            scratch_shapes=[
                pltpu.VMEM((HEADS, BLOCK), F32),
                pltpu.VMEM((GROUPS, BLOCK, PER), F32),
                pltpu.VMEM((GROUPS, BLOCK, PER), F32),
                pltpu.VMEM((BLOCK, BLOCK), F32),
            ],
        ),
        out_shape=[jax.ShapeDtypeStruct(query.shape, F32), jax.ShapeDtypeStruct(query.shape, BF16)],
        compiler_params=pltpu.CompilerParams(vmem_limit_bytes=VMEM),
        cost_estimate=pl.CostEstimate(flops=1_400_000_000, bytes_accessed=16_000_000, transcendentals=2_700_000),
        name="local_attention",
    )(block, query, keyed, valued, decay, docs)

    moved, within, decayed = lax.optimization_barrier((moved, within, decayed))
    vmem = pl.BlockSpec(memory_space=pltpu.VMEM)
    states, decayed = pl.pallas_call(
        scan_kernel,
        in_specs=[pl.BlockSpec(memory_space=pltpu.SMEM), vmem, pl.BlockSpec(memory_space=pltpu.HBM)],
        out_specs=[vmem, vmem],
        out_shape=[jax.ShapeDtypeStruct((DEVICES, PER, 8, DH), BF16), jax.ShapeDtypeStruct(query.shape, BF16)],
        scratch_shapes=[
            pltpu.VMEM((DEVICES * ROWS, DH), F32),
            pltpu.VMEM((DEVICES, PER * DH), F32),
            pltpu.SemaphoreType.DMA,
        ],
        compiler_params=pltpu.CompilerParams(vmem_limit_bytes=16 << 20),
        name="block_scan",
    )(block, moved, pltpu.with_memory_space_constraint(decayed, pltpu.HBM))

    entering = exchange(states)

    return pl.pallas_call(
        finish_kernel,
        in_specs=[vmem] * 4,
        out_specs=pl.BlockSpec(memory_space=pl.ANY),
        out_shape=jax.ShapeDtypeStruct(query.shape, BF16),
        scratch_shapes=[pltpu.VMEM(query.shape, BF16), pltpu.SemaphoreType.DMA((GROUPS,))],
        compiler_params=pltpu.CompilerParams(vmem_limit_bytes=16 << 20),
        name="finish",
    )(decayed, entering, within, gain)


def solution(mesh):
    placed = P(("seq", "head"), None)
    return jax.shard_map(
        body, mesh=mesh, in_specs=(placed, placed, placed, placed, P(), P()), out_specs=placed, check_vma=False
    )
```
